32 devices in a mesh: fsdp: 8 (over z, core), head: 4 (over y, x).
Axes of the slice: x: 2, y: 2, z: 4, core: 2. Of those that a mesh axis runs over, the one named last changes fastest.
Arguments:
- tokens: bfloat16 [2048, 4096], P('fsdp'), may hold values from -6 to 6
- zx_weight: bfloat16 [4096, 128, 128], P('fsdp', 'head'), may hold values from -0.09375 to 0.09375
- dt_weight: bfloat16 [4096, 128], P('fsdp', 'head'), may hold values from -0.09375 to 0.09375
- bc_weight: bfloat16 [4096, 1024], P('fsdp'), may hold values from -0.09375 to 0.09375
- conv_x: float32 [4, 8192], P(None, 'head'), may hold values from -2 to 2
- conv_bc: float32 [4, 1024], replicated, may hold values from -2 to 2
- a_log: float32 [128], P('head'), may hold values from -5 to 0.5
- dt_bias: float32 [128], P('head'), may hold values from -4 to 0
- d_skip: float32 [128], P('head'), may hold values from 0.5 to 2
- norm_gain: float32 [8192], P('head'), may hold values from 0.1 to 1.9
- out_weight: bfloat16 [8192, 4096], P('head'), may hold values from -0.09375 to 0.09375
Outputs:
- mixed: bfloat16 [2048, 4096], P('fsdp', 'head')
The draws below stay inside these ranges and needn't reach their ends.
All inputs are finite; a program needn't handle non-finite values.
Results may differ from the reference program's by a relative error of at most 0.015.
Values may be sent and summed in bfloat16 or wider, within the bound.
A program may use at most 128 MiB of HBM per device.

```python
import jax
import jax.numpy as jnp
from jax import lax

D = 4096
HEADS = 128
P_SIZE = 64
N = 128
G = 4
KCONV = 4
LEN = 256
INNER = 8192
TOKENS = 2048
N_HEAD = 4


def with_spikes(values, rng, source, target, parts, factor):
    owner, partner = [(jnp.arange(values.shape[position]) // (values.shape[position] // parts)).reshape([-1 if axis == position else 1 for axis in range(values.ndim)]) for position in (source, target)]
    chosen = jax.random.permutation(rng, parts)[partner]
    strong = (owner == chosen) | (owner == (partner + parts // 2) % parts)
    return jnp.where(strong, factor * values, values)


def block_scale(stream_key, shape, shards, least, largest):
    loudness = 1.0
    for position, shards_of in shards:
        steps = jax.random.uniform(jax.random.fold_in(jax.random.fold_in(stream_key, 6), position), (shards_of,), jnp.float32, least / len(shards), largest / len(shards))
        loudness = loudness * jnp.repeat(jnp.exp(steps), shape[position] // shards_of).reshape((-1,) + (1,) * (len(shape) - 1 - position))
    return loudness


def normal_values(key, shape, deviation, reach, split=(), kind=jnp.bfloat16):
    entries = deviation * jax.random.normal(key, shape, jnp.float32)
    if split:
        entries = entries * block_scale(key, shape, split, -0.22, 0.18)
    return jnp.clip(entries, -reach, reach).astype(kind)


def bell_draw_with(key, shape, width, bound, split, heavy, dtype=jnp.bfloat16):
    values = width * jax.random.normal(key, shape, jnp.float32)
    if split:
        values = values * block_scale(key, shape, split, -0.22, 0.18)
    return jnp.clip(with_spikes(values, jax.random.fold_in(key, 3), *heavy), -bound, bound).astype(dtype)


def setup_inputs(seed: int = 0) -> dict:
    arg_keys = jax.random.split(jax.random.key(seed), 12)
    return {
        "tokens": normal_values(arg_keys[0], (TOKENS, D), 1.0, 6.0, ((0, 8),)),
        "zx_weight": normal_values(arg_keys[1], (D, HEADS, 2 * P_SIZE), D ** -0.5, 0.09375, ((0, 8), (1, 4))),
        "dt_weight": normal_values(arg_keys[2], (D, HEADS), D ** -0.5, 0.09375, ((0, 8), (1, 4))),
        "bc_weight": normal_values(arg_keys[3], (D, G * 2 * N), D ** -0.5, 0.09375, ((0, 8),)),
        "conv_x": normal_values(arg_keys[4], (KCONV, INNER), 0.5, 2.0, ((1, 4),), jnp.float32),
        "conv_bc": normal_values(arg_keys[5], (KCONV, G * 2 * N), 0.5, 2.0, (), jnp.float32),
        "a_log": jnp.clip(-5.0 + 5.5 * jax.random.uniform(arg_keys[6], (HEADS,), jnp.float32) ** block_scale(arg_keys[6], (HEADS,), ((0, 4),), -0.2, 0.2), -5.0, 0.5),
        "dt_bias": jnp.clip(-4.0 + 4.0 * jax.random.uniform(arg_keys[7], (HEADS,), jnp.float32) ** block_scale(arg_keys[7], (HEADS,), ((0, 4),), -0.2, 0.2), -4.0, 0.0),
        "d_skip": jnp.clip(0.5 + 1.5 * jax.random.uniform(arg_keys[8], (HEADS,), jnp.float32) ** block_scale(arg_keys[8], (HEADS,), ((0, 4),), -0.2, 0.2), 0.5, 2.0),
        "norm_gain": jnp.clip(1.0 + 0.18 * jax.random.normal(arg_keys[9], (INNER,), jnp.float32), 0.1, 1.9),
        "out_weight": bell_draw_with(arg_keys[10], (INNER, D), INNER ** -0.5, 0.09375, ((0, 4),), (0, 1, 4, 2.0)),
    }


def settle(values):
    return lax.optimization_barrier(values.astype(jnp.bfloat16))

def causal(values, kernel):
    columns = values.shape[1]
    seqs = values.reshape(-1, LEN, columns).astype(jnp.float32)
    padded = jnp.pad(seqs, ((0, 0), (KCONV - 1, 0), (0, 0)))
    total = jnp.zeros(seqs.shape, jnp.float32)
    for tap in range(KCONV):
        total = total + kernel[tap].astype(jnp.float32) * padded[:, tap:tap + LEN]
    return settle(jax.nn.silu(total).reshape(-1, columns))

def reference(tokens, zx_weight, dt_weight, bc_weight, conv_x, conv_bc, a_log, dt_bias, d_skip, norm_gain, out_weight):
    flat = zx_weight.reshape(D, HEADS * 2 * P_SIZE)
    zx = settle(jnp.dot(tokens, flat, preferred_element_type=jnp.float32)).reshape(TOKENS, HEADS, 2, P_SIZE)
    gate = zx[:, :, 0, :].astype(jnp.float32).reshape(TOKENS, INNER)
    xin = zx[:, :, 1, :].reshape(TOKENS, INNER)
    dt_raw = settle(jnp.dot(tokens, dt_weight, preferred_element_type=jnp.float32))
    bc_raw = settle(jnp.dot(tokens, bc_weight, preferred_element_type=jnp.float32))
    xconv = causal(xin, conv_x)
    bconv = causal(bc_raw, conv_bc).reshape(TOKENS, G, 2, N)
    steps = jax.nn.softplus(dt_raw.astype(jnp.float32) + dt_bias)
    rates = jnp.exp(a_log)
    count = TOKENS // LEN
    xs = xconv.astype(jnp.float32).reshape(count, LEN, HEADS, P_SIZE)
    bs = bconv[:, :, 0, :].astype(jnp.float32).reshape(count, LEN, G, N)
    cs = bconv[:, :, 1, :].astype(jnp.float32).reshape(count, LEN, G, N)
    ds = steps.reshape(count, LEN, HEADS)
    lower = jnp.arange(LEN)[:, None] >= jnp.arange(LEN)[None, :]

    def one(item):
        xval, bval, cval, dval = item
        cum = jnp.cumsum(-dval * rates, axis=0)
        seg = cum[:, None, :] - cum[None, :, :]
        decay = jnp.exp(jnp.where(lower[:, :, None], seg, -1e+30))
        inner = jnp.einsum('tgn,sgn->gts', cval, bval, precision=lax.Precision.HIGHEST)
        inner = jnp.repeat(inner, HEADS // G, axis=0).transpose(1, 2, 0)
        weights = inner * decay * dval[None, :, :]
        out = jnp.einsum('tsh,shp->thp', weights, xval, precision=lax.Precision.HIGHEST)
        return out + d_skip[None, :, None] * xval
    ys = lax.map(one, (xs, bs, cs, ds)).reshape(TOKENS, INNER)
    gated = ys * jax.nn.silu(gate)
    grouped = gated.reshape(TOKENS, G, INNER // G)
    meansq = lax.optimization_barrier(jnp.mean(grouped * grouped, axis=2, keepdims=True))
    normed = (grouped / jnp.sqrt(meansq + 1e-05)).reshape(TOKENS, INNER) * norm_gain
    normed = normed.astype(jnp.bfloat16)
    block = INNER // N_HEAD

    def accumulate(index, total):
        left = lax.dynamic_slice_in_dim(normed, index * block, block, 1)
        right = lax.dynamic_slice_in_dim(out_weight, index * block, block, 0)
        part = settle(jnp.dot(left, right, preferred_element_type=jnp.float32))
        return total + part.astype(jnp.float32)
    total = lax.fori_loop(0, N_HEAD, accumulate, jnp.zeros((TOKENS, D), jnp.float32))
    return total.astype(jnp.bfloat16)
```

```python
import functools
import math

import jax
import jax.numpy as jnp
from jax import lax
from jax.experimental import pallas as pl
from jax.experimental.pallas import tpu as pltpu
from jax.sharding import PartitionSpec as P

G = 4
LEN = 256
MESH = pl.DeviceIdType.MESH


def settle(values):
    return lax.optimization_barrier(values.astype(jnp.bfloat16))


def remote(src, dst, send, recv, f, h):
    return pltpu.make_async_remote_copy(
        src_ref=src, dst_ref=dst, send_sem=send, recv_sem=recv, device_id=(f, h), device_id_type=MESH
    )


def project_kernel(
    chips, share, chunks, width, tok_ref, w_ref, out_ref, x, wv, buf, stage,
    local_sem, w_sem, own_sem, z_sem, h_sem, s_sem, line_send, line_recv, fin_sem,
):
    f = lax.axis_index("fsdp")
    h = lax.axis_index("head")
    z, c = lax.div(f, 2), lax.rem(f, 2)
    sib = z * 2 + 1 - c
    part = lax.rem(h, share)
    base = h - part
    tok = tok_ref.shape[0]
    depth = w_ref.shape[1]
    cols = w_ref.shape[2]
    rows = 2 * tok // chunks
    piece = tok // share

    barrier = pltpu.get_barrier_semaphore()
    for o in range(1, chips):
        pl.semaphore_signal(barrier, inc=1, device_id=(lax.rem(z + o, chips) * 2 + c, h), device_id_type=MESH)
    pl.semaphore_signal(barrier, inc=1, device_id=(sib, h), device_id_type=MESH)
    for k in range(1, share):
        pl.semaphore_signal(barrier, inc=1, device_id=(f, base + lax.rem(part + k, share)), device_id_type=MESH)
    pl.semaphore_wait(barrier, chips - 1 + 1 + share - 1)

    def spot(chip, core, p):
        return x.at[pl.ds(pl.multiple_of((chip * 2 + core) * tok + p * piece, 16), piece), :]

    def z_copy(o):
        to = lax.rem(z + o, chips)
        src = tok_ref.at[
            pl.ds(pl.multiple_of(part * piece, 16), piece), pl.ds(pl.multiple_of(to * 2 * depth, 128), 2 * depth)
        ]
        return remote(src, spot(z, c, part), z_sem.at[0, o], z_sem.at[1, o], to * 2 + c, h)

    def h_copy(o, k):
        at = spot(lax.rem(z - o + chips, chips), c, part)
        return remote(at, at, h_sem.at[0, o, k], h_sem.at[1, o, k], f, base + lax.rem(part + k, share))

    def s_copy(o, k):
        at = spot(lax.rem(z - o + chips, chips), c, lax.rem(part - k + share, share))
        return remote(at, at, s_sem.at[0, o, k], s_sem.at[1, o, k], sib, h)

    @pl.loop(1, chips)
    def _(o):
        z_copy(o).start()

    mine = tok_ref.at[:, pl.ds(pl.multiple_of(z * 2 * depth, 128), 2 * depth)]
    my_rows = x.at[pl.ds(pl.multiple_of(f * tok, 16), tok), :]
    own = pltpu.make_async_copy(mine, my_rows, local_sem.at[0])
    own.start()
    own_out = remote(mine, my_rows, own_sem.at[0], own_sem.at[1], sib, h)
    own_out.start()
    w_rows = wv.at[pl.ds(pl.multiple_of(c * depth, 16), depth), :]
    w_own = pltpu.make_async_copy(w_ref.at[c], w_rows, local_sem.at[1])
    w_own.start()
    w_out = remote(w_ref.at[1 - c], w_rows, w_sem.at[0], w_sem.at[1], sib, h)
    w_out.start()

    @pl.loop(1, chips)
    def _(o):
        z_copy(o).wait_recv()
        for k in range(1, share):
            h_copy(o, k).start()
        s_copy(o, 0).start()

    @pl.loop(1, chips)
    def _(o):
        for k in range(1, share):
            h_copy(o, k).wait_recv()
            s_copy(o, k).start()

    own.wait()
    w_own.wait()
    own_out.wait()
    w_out.wait()

    @pl.loop(1, chips)
    def _(o):
        z_copy(o).wait_send()
        for k in range(1, share):
            h_copy(o, k).wait_send()
        for k in range(share):
            s_copy(o, k).wait()

    def partial(d, ch, j):
        left = x[pl.ds(pl.multiple_of(d * 2 * tok + ch * rows, 16), rows), :]
        right = wv[:, pl.ds(pl.multiple_of(j * width, 128), width)]
        return jnp.dot(left, right, preferred_element_type=jnp.float32)

    total = (chips - 1) * chunks

    def line(way, d, ch, i):
        to = z + 1 - 2 * way
        at = buf.at[way, d, pl.ds(pl.multiple_of(ch * rows, 16), rows), :]
        return remote(at, at, line_send.at[way, i], line_recv.at[way, i], to * 2 + c, h)

    def where(way, i):
        d = lax.div(i, chunks)
        return (chips - 1 - d if way == 0 else d), lax.rem(i, chunks)

    @pl.loop(0, total)
    def _(i):
        for way in (0, 1):
            d, ch = where(way, i)
            active = z < d if way == 0 else z > d
            first = z == 0 if way == 0 else z == chips - 1

            @pl.when(active)
            def _(way=way, d=d, ch=ch, first=first):
                at = pl.ds(pl.multiple_of(ch * rows, 16), rows)

                @pl.when(jnp.logical_not(first))
                def _():
                    line(way, d, ch, i).wait_recv()

                    @pl.loop(0, cols // width)
                    def _(j):
                        to = pl.ds(pl.multiple_of(j * width, 128), width)
                        got = buf[way, d, at, to].astype(jnp.float32)
                        buf[way, d, at, to] = (got + partial(d, ch, j)).astype(jnp.bfloat16)

                @pl.when(first)
                def _():
                    @pl.loop(0, cols // width)
                    def _(j):
                        to = pl.ds(pl.multiple_of(j * width, 128), width)
                        buf[way, d, at, to] = partial(d, ch, j).astype(jnp.bfloat16)

                @pl.when(i >= 2)
                def _():
                    d2, ch2 = where(way, i - 2)
                    line(way, d2, ch2, i - 2).wait_send()

                line(way, d, ch, i).start()

    half = chunks // 2

    def finish(ch):
        at = stage.at[pl.ds(pl.multiple_of(lax.rem(ch, half) * rows, 16), rows), :]
        to = out_ref.at[c, pl.ds(pl.multiple_of(lax.rem(ch, half) * rows, 16), rows), :]
        return remote(at, to, fin_sem.at[0, lax.rem(ch, half)], fin_sem.at[1, lax.rem(ch, half)], sib, h)

    @pl.loop(0, chunks)
    def _(ch):
        at = pl.ds(pl.multiple_of(ch * rows, 16), rows)

        @pl.when(z > 0)
        def _():
            line(0, z, ch, (chips - 1 - z) * chunks + ch).wait_recv()

        @pl.when(z < chips - 1)
        def _():
            line(1, z, ch, z * chunks + ch).wait_recv()

        here = lax.div(ch, half) == c
        to_rows = pl.ds(pl.multiple_of(lax.rem(ch, half) * rows, 16), rows)

        @pl.loop(0, cols // width)
        def _(j):
            to = pl.ds(pl.multiple_of(j * width, 128), width)
            stage2 = partial(z, ch, j)

            def both(v):
                @pl.when(here)
                def _():
                    out_ref[c, to_rows, to] = v.astype(jnp.bfloat16)

                @pl.when(jnp.logical_not(here))
                def _():
                    stage[to_rows, to] = v.astype(jnp.bfloat16)

            @pl.when(z == 0)
            def _():
                both(stage2 + buf[1, z, at, to].astype(jnp.float32))

            @pl.when(z == chips - 1)
            def _():
                both(stage2 + buf[0, z, at, to].astype(jnp.float32))

            @pl.when(jnp.logical_and(z > 0, z < chips - 1))
            def _():
                both(stage2 + buf[0, z, at, to].astype(jnp.float32) + buf[1, z, at, to].astype(jnp.float32))

        @pl.when(jnp.logical_not(here))
        def _():
            finish(ch).start()

    @pl.loop(0, half)
    def _(ch):
        finish(ch).wait()

    for way in (0, 1):
        count = (chips - 1 - z if way == 0 else z) * chunks

        @pl.when(count > 0)
        def _(way=way, count=count):
            for back in (2, 1):
                d2, ch2 = where(way, count - back)
                line(way, d2, ch2, count - back).wait_send()


def project(tokens, weights, n_fsdp, n_head):
    chips = n_fsdp // 2
    share = math.gcd(n_head, 4)
    tok = tokens.shape[0]
    depth, cols = weights.shape[1:]
    chunks = 4
    width = max(w for w in range(128, 769, 128) if cols % w == 0)
    total = (chips - 1) * chunks
    return pl.pallas_call(
        functools.partial(project_kernel, chips, share, chunks, width),
        out_shape=jax.ShapeDtypeStruct((2, tok, cols), jnp.bfloat16),
        in_specs=[pl.BlockSpec(memory_space=pl.ANY)] * 2,
        out_specs=pl.BlockSpec(memory_space=pltpu.VMEM),
        scratch_shapes=[
            pltpu.VMEM((chips * 2 * tok, 2 * depth), jnp.bfloat16),
            pltpu.VMEM((2 * depth, cols), jnp.bfloat16),
            pltpu.VMEM((2, chips, 2 * tok, cols), jnp.bfloat16),
            pltpu.VMEM((tok, cols), jnp.bfloat16),
            pltpu.SemaphoreType.DMA((2,)),
            pltpu.SemaphoreType.DMA((2,)),
            pltpu.SemaphoreType.DMA((2,)),
            pltpu.SemaphoreType.DMA((2, chips)),
            pltpu.SemaphoreType.DMA((2, chips, share)),
            pltpu.SemaphoreType.DMA((2, chips, share)),
            pltpu.SemaphoreType.DMA((2, total)),
            pltpu.SemaphoreType.DMA((2, total)),
            pltpu.SemaphoreType.DMA((2, chunks // 2)),
        ],
        compiler_params=pltpu.CompilerParams(
            collective_id=0, has_side_effects=True, vmem_limit_bytes=48 * 1024 * 1024
        ),
    )(tokens, weights)


def causal(values, kernel, seq_len):
    columns = values.shape[1]
    seqs = values.reshape(-1, seq_len, columns).astype(jnp.float32)
    taps = kernel.shape[0]
    padded = jnp.pad(seqs, ((0, 0), (taps - 1, 0), (0, 0)))
    total = jnp.zeros(seqs.shape, jnp.float32)
    for tap in range(taps):
        total = total + kernel[tap] * padded[:, tap : tap + seq_len]
    return settle(jax.nn.silu(total).reshape(-1, columns))


def on_device(
    tokens,
    zx_weight,
    dt_weight,
    bc_weight,
    conv_x,
    conv_bc,
    a_log,
    dt_bias,
    d_skip,
    norm_gain,
    out_weight,
):
    tok_rows = tokens.shape[0]
    heads_here = zx_weight.shape[1]
    head_size = zx_weight.shape[2] // 2
    n_head = lax.axis_size("head")
    n_fsdp = lax.axis_size("fsdp")
    head_pos = lax.axis_index("head")
    per_group = n_head // G
    group_id = head_pos // per_group
    group_cols = bc_weight.shape[1] // G
    state = group_cols // 2
    piece_cols = group_cols // per_group
    depth = zx_weight.shape[0]
    bc_part = lax.dynamic_slice_in_dim(bc_weight, head_pos * piece_cols, piece_cols, 1)
    flat_zx = zx_weight.reshape(depth, heads_here * 2 * head_size)
    zx_half, bc_half, dt_half = heads_here * head_size, piece_cols // 2, heads_here // 2
    used = zx_half + bc_half + dt_half
    cols = -(-used // 128) * 128
    blank = jnp.zeros((depth, cols - used), jnp.bfloat16)
    weights = jnp.stack(
        [
            jnp.concatenate(
                [
                    flat_zx[:, c * zx_half : (c + 1) * zx_half],
                    bc_part[:, c * bc_half : (c + 1) * bc_half],
                    dt_weight[:, c * dt_half : (c + 1) * dt_half],
                    blank,
                ],
                axis=1,
            )
            for c in (0, 1)
        ]
    )
    got = project(tokens, weights, n_fsdp, n_head)
    zx = jnp.concatenate([got[0, :, :zx_half], got[1, :, :zx_half]], axis=1).reshape(
        tok_rows, heads_here, 2, head_size
    )
    bc_raw = jnp.concatenate([got[0, :, zx_half : zx_half + bc_half], got[1, :, zx_half : zx_half + bc_half]], axis=1)
    dt_raw = jnp.concatenate([got[0, :, zx_half + bc_half : used], got[1, :, zx_half + bc_half : used]], axis=1)
    if per_group > 1:
        gathered = lax.all_gather(bc_raw, "head", axis=1, tiled=True)
        bc_raw = lax.dynamic_slice_in_dim(gathered, group_id * group_cols, group_cols, 1)
    channels = heads_here * head_size
    gate = zx[:, :, 0, :].astype(jnp.float32).reshape(tok_rows, channels)
    xin = zx[:, :, 1, :].reshape(tok_rows, channels)
    xconv = causal(xin, conv_x, LEN)
    conv_group = lax.dynamic_slice_in_dim(conv_bc, group_id * group_cols, group_cols, 1)
    bconv = causal(bc_raw, conv_group, LEN)
    count = tok_rows // LEN
    steps = jax.nn.softplus(dt_raw.astype(jnp.float32) + dt_bias).reshape(count, LEN, heads_here)
    lower = jnp.arange(LEN)[:, None] >= jnp.arange(LEN)[None, :]
    cum = jnp.einsum(
        "ts,bsh->bth", lower.astype(jnp.float32), -steps * jnp.exp(a_log), precision=lax.Precision.HIGHEST
    )
    seg = cum[:, :, None, :] - cum[:, None, :, :]
    decay = jnp.exp(jnp.where(lower[None, :, :, None], seg, -1e30))
    bseq = bconv[:, :state].reshape(count, LEN, state)
    cseq = bconv[:, state:].reshape(count, LEN, state)
    inner = jnp.einsum("btn,bsn->bts", cseq, bseq, preferred_element_type=jnp.float32)
    weights = inner[..., None] * decay * steps[:, None, :, :]
    xval = xconv.astype(jnp.float32).reshape(count, LEN, heads_here, head_size)
    ys = jnp.einsum("btsh,bshp->bthp", weights, xval, precision=lax.Precision.HIGHEST)
    ys = ys + d_skip[None, None, :, None] * xval
    gated = ys.reshape(tok_rows, channels) * jax.nn.silu(gate)
    local_sq = jnp.sum(gated * gated, axis=1)
    if per_group > 1:
        picks = jnp.arange(G)[None, :] == group_id
        totals = lax.psum(jnp.where(picks, local_sq[:, None], 0.0), "head")
        local_sq = jnp.sum(jnp.where(picks, totals, 0.0), axis=1)
    meansq = local_sq / (per_group * channels)
    normed = (gated / jnp.sqrt(meansq + 1e-05)[:, None] * norm_gain).astype(jnp.bfloat16)
    partial_out = jnp.dot(normed, out_weight, preferred_element_type=jnp.float32)
    return lax.psum_scatter(
        partial_out.astype(jnp.bfloat16), "head", scatter_dimension=1, tiled=True
    )


def solution(mesh):
    in_specs = (
        P("fsdp", None),
        P("fsdp", "head", None),
        P("fsdp", "head"),
        P("fsdp", None),
        P(None, "head"),
        P(),
        P("head"),
        P("head"),
        P("head"),
        P("head"),
        P("head", None),
    )
    out_specs = P("fsdp", "head")
    return jax.shard_map(
        on_device, mesh=mesh, in_specs=in_specs, out_specs=out_specs, check_vma=False
    )
```

```python
import functools
import math

import jax
import jax.numpy as jnp
from jax import lax
from jax.experimental import pallas as pl
from jax.experimental.pallas import tpu as pltpu
from jax.sharding import PartitionSpec as P

G = 4
LEN = 256
MESH = pl.DeviceIdType.MESH


def settle(values):
    return lax.optimization_barrier(values.astype(jnp.bfloat16))


def remote(src, dst, send, recv, f, h):
    return pltpu.make_async_remote_copy(
        src_ref=src, dst_ref=dst, send_sem=send, recv_sem=recv, device_id=(f, h), device_id_type=MESH
    )


def project_kernel(
    chips, share, chunks, width, tok_ref, w_ref, e_ref, out_ref, x, wv, buf, stage,
    local_sem, w_sem, own_sem, z_sem, h_sem, s_sem, line_send, line_recv, fin_sem,
):
    f = lax.axis_index("fsdp")
    h = lax.axis_index("head")
    z, c = lax.div(f, 2), lax.rem(f, 2)
    sib = z * 2 + 1 - c
    part = lax.rem(h, share)
    base = h - part
    tok = tok_ref.shape[0]
    depth = w_ref.shape[0]
    main = w_ref.shape[1] // 2
    cols = main + e_ref.shape[2]
    rows = 2 * tok // chunks
    piece = tok // share

    barrier = pltpu.get_barrier_semaphore()
    for o in range(1, chips):
        pl.semaphore_signal(barrier, inc=1, device_id=(lax.rem(z + o, chips) * 2 + c, h), device_id_type=MESH)
    pl.semaphore_signal(barrier, inc=1, device_id=(sib, h), device_id_type=MESH)
    for k in range(1, share):
        pl.semaphore_signal(barrier, inc=1, device_id=(f, base + lax.rem(part + k, share)), device_id_type=MESH)
    pl.semaphore_wait(barrier, chips - 1 + 1 + share - 1)

    def spot(chip, core, p):
        return x.at[pl.ds(pl.multiple_of((chip * 2 + core) * tok + p * piece, 16), piece), :]

    def z_copy(o):
        to = lax.rem(z + o, chips)
        src = tok_ref.at[
            pl.ds(pl.multiple_of(part * piece, 16), piece), pl.ds(pl.multiple_of(to * 2 * depth, 128), 2 * depth)
        ]
        return remote(src, spot(z, c, part), z_sem.at[0, o], z_sem.at[1, o], to * 2 + c, h)

    def h_copy(o, k):
        at = spot(lax.rem(z - o + chips, chips), c, part)
        return remote(at, at, h_sem.at[0, o, k], h_sem.at[1, o, k], f, base + lax.rem(part + k, share))

    def s_copy(o, k):
        at = spot(lax.rem(z - o + chips, chips), c, lax.rem(part - k + share, share))
        return remote(at, at, s_sem.at[0, o, k], s_sem.at[1, o, k], sib, h)

    @pl.loop(1, chips)
    def _(o):
        z_copy(o).start()

    mine = tok_ref.at[:, pl.ds(pl.multiple_of(z * 2 * depth, 128), 2 * depth)]
    my_rows = x.at[pl.ds(pl.multiple_of(f * tok, 16), tok), :]
    own = pltpu.make_async_copy(mine, my_rows, local_sem.at[0])
    own.start()
    own_out = remote(mine, my_rows, own_sem.at[0], own_sem.at[1], sib, h)
    own_out.start()
    w_rows = pl.ds(pl.multiple_of(c * depth, 16), depth)
    w_main, w_ext = wv.at[w_rows, pl.ds(0, main)], wv.at[w_rows, pl.ds(main, cols - main)]

    def half_of(core):
        return w_ref.at[:, pl.ds(pl.multiple_of(core * main, 128), main)]

    w_own = pltpu.make_async_copy(half_of(c), w_main, local_sem.at[1])
    w_own.start()
    e_own = pltpu.make_async_copy(e_ref.at[c], w_ext, local_sem.at[2])
    e_own.start()
    w_out = remote(half_of(1 - c), w_main, w_sem.at[0], w_sem.at[1], sib, h)
    w_out.start()
    e_out = remote(e_ref.at[1 - c], w_ext, w_sem.at[2], w_sem.at[3], sib, h)
    e_out.start()

    @pl.loop(1, chips)
    def _(o):
        z_copy(o).wait_recv()
        for k in range(1, share):
            h_copy(o, k).start()
        s_copy(o, 0).start()

    @pl.loop(1, chips)
    def _(o):
        for k in range(1, share):
            h_copy(o, k).wait_recv()
            s_copy(o, k).start()

    own.wait()
    w_own.wait()
    e_own.wait()
    own_out.wait()
    w_out.wait()
    e_out.wait()

    @pl.loop(1, chips)
    def _(o):
        z_copy(o).wait_send()
        for k in range(1, share):
            h_copy(o, k).wait_send()
        for k in range(share):
            s_copy(o, k).wait()

    def partial(d, ch, j):
        left = x[pl.ds(pl.multiple_of(d * 2 * tok + ch * rows, 16), rows), :]
        right = wv[:, pl.ds(pl.multiple_of(j * width, 128), width)]
        return jnp.dot(left, right, preferred_element_type=jnp.float32)

    total = (chips - 1) * chunks

    def line(way, d, ch, i):
        to = z + 1 - 2 * way
        at = buf.at[way, d, pl.ds(pl.multiple_of(ch * rows, 16), rows), :]
        return remote(at, at, line_send.at[way, i], line_recv.at[way, i], to * 2 + c, h)

    def where(way, i):
        d = lax.div(i, chunks)
        return (chips - 1 - d if way == 0 else d), lax.rem(i, chunks)

    @pl.loop(0, total)
    def _(i):
        for way in (0, 1):
            d, ch = where(way, i)
            active = z < d if way == 0 else z > d
            first = z == 0 if way == 0 else z == chips - 1

            @pl.when(active)
            def _(way=way, d=d, ch=ch, first=first):
                at = pl.ds(pl.multiple_of(ch * rows, 16), rows)

                @pl.when(jnp.logical_not(first))
                def _():
                    line(way, d, ch, i).wait_recv()

                    @pl.loop(0, cols // width)
                    def _(j):
                        to = pl.ds(pl.multiple_of(j * width, 128), width)
                        got = buf[way, d, at, to].astype(jnp.float32)
                        buf[way, d, at, to] = (got + partial(d, ch, j)).astype(jnp.bfloat16)

                @pl.when(first)
                def _():
                    @pl.loop(0, cols // width)
                    def _(j):
                        to = pl.ds(pl.multiple_of(j * width, 128), width)
                        buf[way, d, at, to] = partial(d, ch, j).astype(jnp.bfloat16)

                @pl.when(i >= 2)
                def _():
                    d2, ch2 = where(way, i - 2)
                    line(way, d2, ch2, i - 2).wait_send()

                line(way, d, ch, i).start()

    half = chunks // 2

    def finish(ch):
        at = stage.at[pl.ds(pl.multiple_of(lax.rem(ch, half) * rows, 16), rows), :]
        to = out_ref.at[c, pl.ds(pl.multiple_of(lax.rem(ch, half) * rows, 16), rows), :]
        return remote(at, to, fin_sem.at[0, lax.rem(ch, half)], fin_sem.at[1, lax.rem(ch, half)], sib, h)

    @pl.loop(0, chunks)
    def _(ch):
        at = pl.ds(pl.multiple_of(ch * rows, 16), rows)

        @pl.when(z > 0)
        def _():
            line(0, z, ch, (chips - 1 - z) * chunks + ch).wait_recv()

        @pl.when(z < chips - 1)
        def _():
            line(1, z, ch, z * chunks + ch).wait_recv()

        here = lax.div(ch, half) == c
        to_rows = pl.ds(pl.multiple_of(lax.rem(ch, half) * rows, 16), rows)

        @pl.loop(0, cols // width)
        def _(j):
            to = pl.ds(pl.multiple_of(j * width, 128), width)
            stage2 = partial(z, ch, j)

            def both(v):
                @pl.when(here)
                def _():
                    out_ref[c, to_rows, to] = v.astype(jnp.bfloat16)

                @pl.when(jnp.logical_not(here))
                def _():
                    stage[to_rows, to] = v.astype(jnp.bfloat16)

            @pl.when(z == 0)
            def _():
                both(stage2 + buf[1, z, at, to].astype(jnp.float32))

            @pl.when(z == chips - 1)
            def _():
                both(stage2 + buf[0, z, at, to].astype(jnp.float32))

            @pl.when(jnp.logical_and(z > 0, z < chips - 1))
            def _():
                both(stage2 + buf[0, z, at, to].astype(jnp.float32) + buf[1, z, at, to].astype(jnp.float32))

        @pl.when(jnp.logical_not(here))
        def _():
            finish(ch).start()

    @pl.loop(0, half)
    def _(ch):
        finish(ch).wait()

    for way in (0, 1):
        count = (chips - 1 - z if way == 0 else z) * chunks

        @pl.when(count > 0)
        def _(way=way, count=count):
            for back in (2, 1):
                d2, ch2 = where(way, count - back)
                line(way, d2, ch2, count - back).wait_send()


def project(tokens, weights, extra, n_fsdp, n_head):
    chips = n_fsdp // 2
    share = math.gcd(n_head, 4)
    tok = tokens.shape[0]
    depth = weights.shape[0]
    cols = weights.shape[1] // 2 + extra.shape[2]
    chunks = 4
    width = max(w for w in range(128, 769, 128) if cols % w == 0)
    total = (chips - 1) * chunks
    return pl.pallas_call(
        functools.partial(project_kernel, chips, share, chunks, width),
        out_shape=jax.ShapeDtypeStruct((2, tok, cols), jnp.bfloat16),
        in_specs=[pl.BlockSpec(memory_space=pl.ANY)] * 3,
        out_specs=pl.BlockSpec(memory_space=pltpu.VMEM),
        scratch_shapes=[
            pltpu.VMEM((chips * 2 * tok, 2 * depth), jnp.bfloat16),
            pltpu.VMEM((2 * depth, cols), jnp.bfloat16),
            pltpu.VMEM((2, chips, 2 * tok, cols), jnp.bfloat16),
            pltpu.VMEM((tok, cols), jnp.bfloat16),
            pltpu.SemaphoreType.DMA((3,)),
            pltpu.SemaphoreType.DMA((4,)),
            pltpu.SemaphoreType.DMA((2,)),
            pltpu.SemaphoreType.DMA((2, chips)),
            pltpu.SemaphoreType.DMA((2, chips, share)),
            pltpu.SemaphoreType.DMA((2, chips, share)),
            pltpu.SemaphoreType.DMA((2, total)),
            pltpu.SemaphoreType.DMA((2, total)),
            pltpu.SemaphoreType.DMA((2, chunks // 2)),
        ],
        compiler_params=pltpu.CompilerParams(
            collective_id=0, has_side_effects=True, vmem_limit_bytes=48 * 1024 * 1024
        ),
    )(tokens, weights, extra)


def out_kernel(peers, width, n_ref, w_ref, out_ref, wbuf, held, landed, w_sem, send_sem, recv_sem):
    f = lax.axis_index("fsdp")
    h = lax.axis_index("head")
    block = out_ref.shape[1]

    def w_copy(o):
        to = lax.rem(h + o, peers)
        at = w_ref.at[:, pl.ds(pl.multiple_of(to * block, 128), block)]
        return pltpu.make_async_copy(at, wbuf.at[o], w_sem.at[o])

    def send(o):
        return remote(held.at[o], landed.at[o], send_sem.at[o], recv_sem.at[o], f, lax.rem(h + o, peers))

    for o in range(1, peers):
        w_copy(o).start()
    w_copy(0).start()
    barrier = pltpu.get_barrier_semaphore()
    for o in range(1, peers):
        pl.semaphore_signal(barrier, inc=1, device_id=(f, lax.rem(h + o, peers)), device_id_type=MESH)
    pl.semaphore_wait(barrier, peers - 1)

    def columns(o, j):
        to = pl.ds(pl.multiple_of(j * width, 128), width)
        return to, jnp.dot(n_ref[...], wbuf[o, :, to], preferred_element_type=jnp.float32).astype(jnp.bfloat16)

    @pl.loop(1, peers)
    def _(o):
        w_copy(o).wait()

        @pl.loop(0, block // width)
        def _(j):
            to, value = columns(o, j)
            held[o, :, to] = value

        send(o).start()

    w_copy(0).wait()

    @pl.loop(0, block // width)
    def _(j):
        to, value = columns(0, j)
        held[0, :, to] = value

    @pl.loop(1, peers)
    def _(o):
        send(o).wait()

    @pl.loop(0, block // width)
    def _(j):
        to = pl.ds(pl.multiple_of(j * width, 128), width)
        total = held[0, :, to].astype(jnp.float32)
        for o in range(1, peers):
            total = total + landed[o, :, to].astype(jnp.float32)
        out_ref[:, to] = total.astype(jnp.bfloat16)


def out_project(normed, weight, n_head):
    tok, rows = normed.shape
    block = weight.shape[1] // n_head
    width = 256 if block % 256 == 0 else 128
    return pl.pallas_call(
        functools.partial(out_kernel, n_head, width),
        out_shape=jax.ShapeDtypeStruct((tok, block), jnp.bfloat16),
        in_specs=[pl.BlockSpec(memory_space=pltpu.VMEM), pl.BlockSpec(memory_space=pl.ANY)],
        out_specs=pl.BlockSpec(memory_space=pltpu.VMEM),
        scratch_shapes=[
            pltpu.VMEM((n_head, rows, block), jnp.bfloat16),
            pltpu.VMEM((n_head, tok, block), jnp.bfloat16),
            pltpu.VMEM((n_head, tok, block), jnp.bfloat16),
            pltpu.SemaphoreType.DMA((n_head,)),
            pltpu.SemaphoreType.DMA((n_head,)),
            pltpu.SemaphoreType.DMA((n_head,)),
        ],
        compiler_params=pltpu.CompilerParams(
            collective_id=1, has_side_effects=True, vmem_limit_bytes=40 * 1024 * 1024
        ),
    )(normed, weight)


def causal(values, kernel, seq_len):
    columns = values.shape[1]
    seqs = values.reshape(-1, seq_len, columns).astype(jnp.float32)
    taps = kernel.shape[0]
    padded = jnp.pad(seqs, ((0, 0), (taps - 1, 0), (0, 0)))
    total = jnp.zeros(seqs.shape, jnp.float32)
    for tap in range(taps):
        total = total + kernel[tap] * padded[:, tap : tap + seq_len]
    return settle(jax.nn.silu(total).reshape(-1, columns))


def on_device(
    tokens,
    zx_weight,
    dt_weight,
    bc_weight,
    conv_x,
    conv_bc,
    a_log,
    dt_bias,
    d_skip,
    norm_gain,
    out_weight,
):
    tok_rows = tokens.shape[0]
    heads_here = zx_weight.shape[1]
    head_size = zx_weight.shape[2] // 2
    n_head = lax.axis_size("head")
    n_fsdp = lax.axis_size("fsdp")
    head_pos = lax.axis_index("head")
    per_group = n_head // G
    group_id = head_pos // per_group
    group_cols = bc_weight.shape[1] // G
    state = group_cols // 2
    piece_cols = group_cols // per_group
    depth = zx_weight.shape[0]
    bc_part = lax.dynamic_slice_in_dim(bc_weight, head_pos * piece_cols, piece_cols, 1)
    flat_zx = zx_weight.reshape(depth, heads_here * 2 * head_size)
    zx_half, bc_half, dt_half = heads_here * head_size, piece_cols // 2, heads_here // 2
    used = zx_half + bc_half + dt_half
    cols = -(-used // 128) * 128
    blank = jnp.zeros((depth, cols - used), jnp.bfloat16)
    extra = jnp.stack(
        [
            jnp.concatenate(
                [
                    bc_part[:, c * bc_half : (c + 1) * bc_half],
                    dt_weight[:, c * dt_half : (c + 1) * dt_half],
                    blank,
                ],
                axis=1,
            )
            for c in (0, 1)
        ]
    )
    got = project(tokens, flat_zx, extra, n_fsdp, n_head)
    zx = jnp.concatenate([got[0, :, :zx_half], got[1, :, :zx_half]], axis=1).reshape(
        tok_rows, heads_here, 2, head_size
    )
    bc_raw = jnp.concatenate([got[0, :, zx_half : zx_half + bc_half], got[1, :, zx_half : zx_half + bc_half]], axis=1)
    dt_raw = jnp.concatenate([got[0, :, zx_half + bc_half : used], got[1, :, zx_half + bc_half : used]], axis=1)
    if per_group > 1:
        gathered = lax.all_gather(bc_raw, "head", axis=1, tiled=True)
        bc_raw = lax.dynamic_slice_in_dim(gathered, group_id * group_cols, group_cols, 1)
    channels = heads_here * head_size
    gate = zx[:, :, 0, :].astype(jnp.float32).reshape(tok_rows, channels)
    xin = zx[:, :, 1, :].reshape(tok_rows, channels)
    xconv = causal(xin, conv_x, LEN)
    conv_group = lax.dynamic_slice_in_dim(conv_bc, group_id * group_cols, group_cols, 1)
    bconv = causal(bc_raw, conv_group, LEN)
    count = tok_rows // LEN
    steps = jax.nn.softplus(dt_raw.astype(jnp.float32) + dt_bias).reshape(count, LEN, heads_here)
    lower = jnp.arange(LEN)[:, None] >= jnp.arange(LEN)[None, :]
    cum = jnp.einsum(
        "ts,bsh->bth", lower.astype(jnp.float32), -steps * jnp.exp(a_log), precision=lax.Precision.HIGHEST
    )
    seg = cum[:, :, None, :] - cum[:, None, :, :]
    decay = jnp.exp(jnp.where(lower[None, :, :, None], seg, -1e30))
    bseq = bconv[:, :state].reshape(count, LEN, state)
    cseq = bconv[:, state:].reshape(count, LEN, state)
    inner = jnp.einsum("btn,bsn->bts", cseq, bseq, preferred_element_type=jnp.float32)
    weights = inner[..., None] * decay * steps[:, None, :, :]
    xval = xconv.astype(jnp.float32).reshape(count, LEN, heads_here, head_size)
    ys = jnp.einsum("btsh,bshp->bthp", weights, xval, precision=lax.Precision.HIGHEST)
    ys = ys + d_skip[None, None, :, None] * xval
    gated = ys.reshape(tok_rows, channels) * jax.nn.silu(gate)
    local_sq = jnp.sum(gated * gated, axis=1)
    if per_group > 1:
        picks = jnp.arange(G)[None, :] == group_id
        totals = lax.psum(jnp.where(picks, local_sq[:, None], 0.0), "head")
        local_sq = jnp.sum(jnp.where(picks, totals, 0.0), axis=1)
    meansq = local_sq / (per_group * channels)
    normed = (gated / jnp.sqrt(meansq + 1e-05)[:, None] * norm_gain).astype(jnp.bfloat16)
    return out_project(normed, out_weight, n_head)


def solution(mesh):
    in_specs = (
        P("fsdp", None),
        P("fsdp", "head", None),
        P("fsdp", "head"),
        P("fsdp", None),
        P(None, "head"),
        P(),
        P("head"),
        P("head"),
        P("head"),
        P("head"),
        P("head", None),
    )
    out_specs = P("fsdp", "head")
    return jax.shard_map(
        on_device, mesh=mesh, in_specs=in_specs, out_specs=out_specs, check_vma=False
    )
```

```python
import functools
import math

import jax
import jax.numpy as jnp
from jax import lax
from jax.experimental import pallas as pl
from jax.experimental.pallas import tpu as pltpu
from jax.sharding import PartitionSpec as P

G = 4
LEN = 256
MESH = pl.DeviceIdType.MESH


def settle(values):
    return lax.optimization_barrier(values.astype(jnp.bfloat16))


def remote(src, dst, send, recv, f, h):
    return pltpu.make_async_remote_copy(
        src_ref=src, dst_ref=dst, send_sem=send, recv_sem=recv, device_id=(f, h), device_id_type=MESH
    )


def project_kernel(
    chips, share, chunks, width, tok_ref, w_ref, e_ref, out_ref, x, wv, buf, stage,
    local_sem, w_sem, own_sem, z_sem, h_sem, s_sem, line_send, line_recv, fin_sem,
):
    f = lax.axis_index("fsdp")
    h = lax.axis_index("head")
    z, c = lax.div(f, 2), lax.rem(f, 2)
    sib = z * 2 + 1 - c
    part = lax.rem(h, share)
    base = h - part
    tok = tok_ref.shape[0]
    depth = w_ref.shape[0]
    main = w_ref.shape[1] // 2
    cols = main + e_ref.shape[2]
    rows = 2 * tok // chunks
    piece = tok // share

    barrier = pltpu.get_barrier_semaphore()
    for o in range(1, chips):
        pl.semaphore_signal(barrier, inc=1, device_id=(lax.rem(z + o, chips) * 2 + c, h), device_id_type=MESH)
    pl.semaphore_signal(barrier, inc=1, device_id=(sib, h), device_id_type=MESH)
    for k in range(1, share):
        pl.semaphore_signal(barrier, inc=1, device_id=(f, base + lax.rem(part + k, share)), device_id_type=MESH)
    pl.semaphore_wait(barrier, chips - 1 + 1 + share - 1)

    def spot(chip, core, p):
        return x.at[pl.ds(pl.multiple_of((chip * 2 + core) * tok + p * piece, 16), piece), :]

    def z_copy(o):
        to = lax.rem(z + o, chips)
        src = tok_ref.at[
            pl.ds(pl.multiple_of(part * piece, 16), piece), pl.ds(pl.multiple_of(to * 2 * depth, 128), 2 * depth)
        ]
        return remote(src, spot(z, c, part), z_sem.at[0, o], z_sem.at[1, o], to * 2 + c, h)

    def h_copy(o, k):
        at = spot(lax.rem(z - o + chips, chips), c, part)
        return remote(at, at, h_sem.at[0, o, k], h_sem.at[1, o, k], f, base + lax.rem(part + k, share))

    def s_copy(o, k):
        at = spot(lax.rem(z - o + chips, chips), c, lax.rem(part - k + share, share))
        return remote(at, at, s_sem.at[0, o, k], s_sem.at[1, o, k], sib, h)

    @pl.loop(1, chips)
    def _(o):
        z_copy(o).start()

    mine = tok_ref.at[:, pl.ds(pl.multiple_of(z * 2 * depth, 128), 2 * depth)]
    my_rows = x.at[pl.ds(pl.multiple_of(f * tok, 16), tok), :]
    own = pltpu.make_async_copy(mine, my_rows, local_sem.at[0])
    own.start()
    own_out = remote(mine, my_rows, own_sem.at[0], own_sem.at[1], sib, h)
    own_out.start()
    w_rows = pl.ds(pl.multiple_of(c * depth, 16), depth)
    w_main, w_ext = wv.at[w_rows, pl.ds(0, main)], wv.at[w_rows, pl.ds(main, cols - main)]

    def half_of(core):
        return w_ref.at[:, pl.ds(pl.multiple_of(core * main, 128), main)]

    w_own = pltpu.make_async_copy(half_of(c), w_main, local_sem.at[1])
    w_own.start()
    e_own = pltpu.make_async_copy(e_ref.at[c], w_ext, local_sem.at[2])
    e_own.start()
    w_out = remote(half_of(1 - c), w_main, w_sem.at[0], w_sem.at[1], sib, h)
    w_out.start()
    e_out = remote(e_ref.at[1 - c], w_ext, w_sem.at[2], w_sem.at[3], sib, h)
    e_out.start()

    @pl.loop(1, chips)
    def _(o):
        z_copy(o).wait_recv()
        for k in range(1, share):
            h_copy(o, k).start()
        s_copy(o, 0).start()

    @pl.loop(1, chips)
    def _(o):
        for k in range(1, share):
            h_copy(o, k).wait_recv()
            s_copy(o, k).start()

    own.wait()
    w_own.wait()
    e_own.wait()
    own_out.wait()
    w_out.wait()
    e_out.wait()

    @pl.loop(1, chips)
    def _(o):
        z_copy(o).wait_send()
        for k in range(1, share):
            h_copy(o, k).wait_send()
        for k in range(share):
            s_copy(o, k).wait()

    def partial(d, ch, j):
        left = x[pl.ds(pl.multiple_of(d * 2 * tok + ch * rows, 16), rows), :]
        right = wv[:, pl.ds(pl.multiple_of(j * width, 128), width)]
        return jnp.dot(left, right, preferred_element_type=jnp.float32)

    total = (chips - 1) * chunks

    def line(way, d, ch, i):
        to = z + 1 - 2 * way
        at = buf.at[way, d, pl.ds(pl.multiple_of(ch * rows, 16), rows), :]
        return remote(at, at, line_send.at[way, i], line_recv.at[way, i], to * 2 + c, h)

    def where(way, i):
        d = lax.div(i, chunks)
        return (chips - 1 - d if way == 0 else d), lax.rem(i, chunks)

    @pl.loop(0, total)
    def _(i):
        for way in (0, 1):
            d, ch = where(way, i)
            active = z < d if way == 0 else z > d
            first = z == 0 if way == 0 else z == chips - 1

            @pl.when(active)
            def _(way=way, d=d, ch=ch, first=first):
                at = pl.ds(pl.multiple_of(ch * rows, 16), rows)

                @pl.when(jnp.logical_not(first))
                def _():
                    line(way, d, ch, i).wait_recv()

                    @pl.loop(0, cols // width)
                    def _(j):
                        to = pl.ds(pl.multiple_of(j * width, 128), width)
                        got = buf[way, d, at, to].astype(jnp.float32)
                        buf[way, d, at, to] = (got + partial(d, ch, j)).astype(jnp.bfloat16)

                @pl.when(first)
                def _():
                    @pl.loop(0, cols // width)
                    def _(j):
                        to = pl.ds(pl.multiple_of(j * width, 128), width)
                        buf[way, d, at, to] = partial(d, ch, j).astype(jnp.bfloat16)

                @pl.when(i >= 2)
                def _():
                    d2, ch2 = where(way, i - 2)
                    line(way, d2, ch2, i - 2).wait_send()

                line(way, d, ch, i).start()

    half = chunks // 2

    def finish(ch):
        at = stage.at[pl.ds(pl.multiple_of(lax.rem(ch, half) * rows, 16), rows), :]
        to = out_ref.at[c, pl.ds(pl.multiple_of(lax.rem(ch, half) * rows, 16), rows), :]
        return remote(at, to, fin_sem.at[0, lax.rem(ch, half)], fin_sem.at[1, lax.rem(ch, half)], sib, h)

    @pl.loop(0, chunks)
    def _(ch):
        at = pl.ds(pl.multiple_of(ch * rows, 16), rows)

        @pl.when(z > 0)
        def _():
            line(0, z, ch, (chips - 1 - z) * chunks + ch).wait_recv()

        @pl.when(z < chips - 1)
        def _():
            line(1, z, ch, z * chunks + ch).wait_recv()

        here = lax.div(ch, half) == c
        to_rows = pl.ds(pl.multiple_of(lax.rem(ch, half) * rows, 16), rows)

        @pl.loop(0, cols // width)
        def _(j):
            to = pl.ds(pl.multiple_of(j * width, 128), width)
            stage2 = partial(z, ch, j)

            def both(v):
                @pl.when(here)
                def _():
                    out_ref[c, to_rows, to] = v.astype(jnp.bfloat16)

                @pl.when(jnp.logical_not(here))
                def _():
                    stage[to_rows, to] = v.astype(jnp.bfloat16)

            @pl.when(z == 0)
            def _():
                both(stage2 + buf[1, z, at, to].astype(jnp.float32))

            @pl.when(z == chips - 1)
            def _():
                both(stage2 + buf[0, z, at, to].astype(jnp.float32))

            @pl.when(jnp.logical_and(z > 0, z < chips - 1))
            def _():
                both(stage2 + buf[0, z, at, to].astype(jnp.float32) + buf[1, z, at, to].astype(jnp.float32))

        @pl.when(jnp.logical_not(here))
        def _():
            finish(ch).start()

    @pl.loop(0, half)
    def _(ch):
        finish(ch).wait()

    for way in (0, 1):
        count = (chips - 1 - z if way == 0 else z) * chunks

        @pl.when(count > 0)
        def _(way=way, count=count):
            for back in (2, 1):
                d2, ch2 = where(way, count - back)
                line(way, d2, ch2, count - back).wait_send()


def project(tokens, weights, extra, n_fsdp, n_head):
    chips = n_fsdp // 2
    share = math.gcd(n_head, 4)
    tok = tokens.shape[0]
    depth = weights.shape[0]
    cols = weights.shape[1] // 2 + extra.shape[2]
    chunks = 8
    width = max(w for w in range(128, 769, 128) if cols % w == 0)
    total = (chips - 1) * chunks
    return pl.pallas_call(
        functools.partial(project_kernel, chips, share, chunks, width),
        out_shape=jax.ShapeDtypeStruct((2, tok, cols), jnp.bfloat16),
        in_specs=[pl.BlockSpec(memory_space=pl.ANY)] * 3,
        out_specs=pl.BlockSpec(memory_space=pltpu.VMEM),
        scratch_shapes=[
            pltpu.VMEM((chips * 2 * tok, 2 * depth), jnp.bfloat16),
            pltpu.VMEM((2 * depth, cols), jnp.bfloat16),
            pltpu.VMEM((2, chips, 2 * tok, cols), jnp.bfloat16),
            pltpu.VMEM((tok, cols), jnp.bfloat16),
            pltpu.SemaphoreType.DMA((3,)),
            pltpu.SemaphoreType.DMA((4,)),
            pltpu.SemaphoreType.DMA((2,)),
            pltpu.SemaphoreType.DMA((2, chips)),
            pltpu.SemaphoreType.DMA((2, chips, share)),
            pltpu.SemaphoreType.DMA((2, chips, share)),
            pltpu.SemaphoreType.DMA((2, total)),
            pltpu.SemaphoreType.DMA((2, total)),
            pltpu.SemaphoreType.DMA((2, chunks // 2)),
        ],
        compiler_params=pltpu.CompilerParams(
            collective_id=0, has_side_effects=True, vmem_limit_bytes=48 * 1024 * 1024
        ),
    )(tokens, weights, extra)


def out_kernel(peers, width, n_ref, w_ref, out_ref, wbuf, held, landed, w_sem, send_sem, recv_sem):
    f = lax.axis_index("fsdp")
    h = lax.axis_index("head")
    block = out_ref.shape[1]

    def w_copy(o):
        to = lax.rem(h + o, peers)
        at = w_ref.at[:, pl.ds(pl.multiple_of(to * block, 128), block)]
        return pltpu.make_async_copy(at, wbuf.at[o], w_sem.at[o])

    def send(o):
        return remote(held.at[o], landed.at[o], send_sem.at[o], recv_sem.at[o], f, lax.rem(h + o, peers))

    for o in range(1, peers):
        w_copy(o).start()
    w_copy(0).start()
    barrier = pltpu.get_barrier_semaphore()
    for o in range(1, peers):
        pl.semaphore_signal(barrier, inc=1, device_id=(f, lax.rem(h + o, peers)), device_id_type=MESH)
    pl.semaphore_wait(barrier, peers - 1)

    def columns(o, j):
        to = pl.ds(pl.multiple_of(j * width, 128), width)
        return to, jnp.dot(n_ref[...], wbuf[o, :, to], preferred_element_type=jnp.float32).astype(jnp.bfloat16)

    @pl.loop(1, peers)
    def _(o):
        w_copy(o).wait()

        @pl.loop(0, block // width)
        def _(j):
            to, value = columns(o, j)
            held[o, :, to] = value

        send(o).start()

    w_copy(0).wait()

    @pl.loop(0, block // width)
    def _(j):
        to, value = columns(0, j)
        held[0, :, to] = value

    @pl.loop(1, peers)
    def _(o):
        send(o).wait()

    @pl.loop(0, block // width)
    def _(j):
        to = pl.ds(pl.multiple_of(j * width, 128), width)
        total = held[0, :, to].astype(jnp.float32)
        for o in range(1, peers):
            total = total + landed[o, :, to].astype(jnp.float32)
        out_ref[:, to] = total.astype(jnp.bfloat16)


def out_project(normed, weight, n_head):
    tok, rows = normed.shape
    block = weight.shape[1] // n_head
    width = 256 if block % 256 == 0 else 128
    return pl.pallas_call(
        functools.partial(out_kernel, n_head, width),
        out_shape=jax.ShapeDtypeStruct((tok, block), jnp.bfloat16),
        in_specs=[pl.BlockSpec(memory_space=pltpu.VMEM), pl.BlockSpec(memory_space=pl.ANY)],
        out_specs=pl.BlockSpec(memory_space=pltpu.VMEM),
        scratch_shapes=[
            pltpu.VMEM((n_head, rows, block), jnp.bfloat16),
            pltpu.VMEM((n_head, tok, block), jnp.bfloat16),
            pltpu.VMEM((n_head, tok, block), jnp.bfloat16),
            pltpu.SemaphoreType.DMA((n_head,)),
            pltpu.SemaphoreType.DMA((n_head,)),
            pltpu.SemaphoreType.DMA((n_head,)),
        ],
        compiler_params=pltpu.CompilerParams(
            collective_id=1, has_side_effects=True, vmem_limit_bytes=40 * 1024 * 1024
        ),
    )(normed, weight)


def causal(values, kernel, seq_len):
    columns = values.shape[1]
    seqs = values.reshape(-1, seq_len, columns).astype(jnp.float32)
    taps = kernel.shape[0]
    padded = jnp.pad(seqs, ((0, 0), (taps - 1, 0), (0, 0)))
    total = jnp.zeros(seqs.shape, jnp.float32)
    for tap in range(taps):
        total = total + kernel[tap] * padded[:, tap : tap + seq_len]
    return settle(jax.nn.silu(total).reshape(-1, columns))


def on_device(
    tokens,
    zx_weight,
    dt_weight,
    bc_weight,
    conv_x,
    conv_bc,
    a_log,
    dt_bias,
    d_skip,
    norm_gain,
    out_weight,
):
    tok_rows = tokens.shape[0]
    heads_here = zx_weight.shape[1]
    head_size = zx_weight.shape[2] // 2
    n_head = lax.axis_size("head")
    n_fsdp = lax.axis_size("fsdp")
    head_pos = lax.axis_index("head")
    per_group = n_head // G
    group_id = head_pos // per_group
    group_cols = bc_weight.shape[1] // G
    state = group_cols // 2
    piece_cols = group_cols // per_group
    depth = zx_weight.shape[0]
    bc_part = lax.dynamic_slice_in_dim(bc_weight, head_pos * piece_cols, piece_cols, 1)
    flat_zx = zx_weight.reshape(depth, heads_here * 2 * head_size)
    zx_half, bc_half, dt_half = heads_here * head_size, piece_cols // 2, heads_here // 2
    used = zx_half + bc_half + dt_half
    cols = -(-used // 128) * 128
    blank = jnp.zeros((depth, cols - used), jnp.bfloat16)
    extra = jnp.stack(
        [
            jnp.concatenate(
                [
                    bc_part[:, c * bc_half : (c + 1) * bc_half],
                    dt_weight[:, c * dt_half : (c + 1) * dt_half],
                    blank,
                ],
                axis=1,
            )
            for c in (0, 1)
        ]
    )
    got = project(tokens, flat_zx, extra, n_fsdp, n_head)
    zx = jnp.concatenate([got[0, :, :zx_half], got[1, :, :zx_half]], axis=1).reshape(
        tok_rows, heads_here, 2, head_size
    )
    bc_raw = jnp.concatenate([got[0, :, zx_half : zx_half + bc_half], got[1, :, zx_half : zx_half + bc_half]], axis=1)
    dt_raw = jnp.concatenate([got[0, :, zx_half + bc_half : used], got[1, :, zx_half + bc_half : used]], axis=1)
    if per_group > 1:
        gathered = lax.all_gather(bc_raw, "head", axis=1, tiled=True)
        bc_raw = lax.dynamic_slice_in_dim(gathered, group_id * group_cols, group_cols, 1)
    channels = heads_here * head_size
    gate = zx[:, :, 0, :].astype(jnp.float32).reshape(tok_rows, channels)
    xin = zx[:, :, 1, :].reshape(tok_rows, channels)
    xconv = causal(xin, conv_x, LEN)
    conv_group = lax.dynamic_slice_in_dim(conv_bc, group_id * group_cols, group_cols, 1)
    bconv = causal(bc_raw, conv_group, LEN)
    count = tok_rows // LEN
    steps = jax.nn.softplus(dt_raw.astype(jnp.float32) + dt_bias).reshape(count, LEN, heads_here)
    lower = jnp.arange(LEN)[:, None] >= jnp.arange(LEN)[None, :]
    cum = jnp.einsum(
        "ts,bsh->bth", lower.astype(jnp.float32), -steps * jnp.exp(a_log), precision=lax.Precision.HIGHEST
    )
    seg = cum[:, :, None, :] - cum[:, None, :, :]
    decay = jnp.exp(jnp.where(lower[None, :, :, None], seg, -1e30))
    bseq = bconv[:, :state].reshape(count, LEN, state)
    cseq = bconv[:, state:].reshape(count, LEN, state)
    inner = jnp.einsum("btn,bsn->bts", cseq, bseq, preferred_element_type=jnp.float32)
    weights = inner[..., None] * decay * steps[:, None, :, :]
    xval = xconv.astype(jnp.float32).reshape(count, LEN, heads_here, head_size)
    xbf = xconv.reshape(count, LEN, heads_here, head_size)
    ys = jnp.einsum("btsh,bshp->bthp", weights.astype(jnp.bfloat16), xbf, preferred_element_type=jnp.float32)
    ys = ys + d_skip[None, None, :, None] * xval
    gated = ys.reshape(tok_rows, channels) * jax.nn.silu(gate)
    local_sq = jnp.sum(gated * gated, axis=1)
    if per_group > 1:
        picks = jnp.arange(G)[None, :] == group_id
        totals = lax.psum(jnp.where(picks, local_sq[:, None], 0.0), "head")
        local_sq = jnp.sum(jnp.where(picks, totals, 0.0), axis=1)
    meansq = local_sq / (per_group * channels)
    normed = (gated / jnp.sqrt(meansq + 1e-05)[:, None] * norm_gain).astype(jnp.bfloat16)
    return out_project(normed, out_weight, n_head)


def solution(mesh):
    in_specs = (
        P("fsdp", None),
        P("fsdp", "head", None),
        P("fsdp", "head"),
        P("fsdp", None),
        P(None, "head"),
        P(),
        P("head"),
        P("head"),
        P("head"),
        P("head"),
        P("head", None),
    )
    out_specs = P("fsdp", "head")
    return jax.shard_map(
        on_device, mesh=mesh, in_specs=in_specs, out_specs=out_specs, check_vma=False
    )
```

```python
import functools
import math

import jax
import jax.numpy as jnp
from jax import lax
from jax.experimental import pallas as pl
from jax.experimental.pallas import tpu as pltpu
from jax.sharding import PartitionSpec as P

G = 4
LEN = 256
MESH = pl.DeviceIdType.MESH


def settle(values):
    return lax.optimization_barrier(values.astype(jnp.bfloat16))


def remote(src, dst, send, recv, f, h):
    return pltpu.make_async_remote_copy(
        src_ref=src, dst_ref=dst, send_sem=send, recv_sem=recv, device_id=(f, h), device_id_type=MESH
    )


def project_kernel(
    chips, share, chunks, width, tok_ref, w_ref, e_ref, out_ref, x, wv, buf, stage,
    local_sem, w_sem, own_sem, z_sem, h_sem, s_sem, line_send, line_recv, fin_sem,
):
    f = lax.axis_index("fsdp")
    h = lax.axis_index("head")
    z, c = lax.div(f, 2), lax.rem(f, 2)
    sib = z * 2 + 1 - c
    part = lax.rem(h, share)
    base = h - part
    tok = tok_ref.shape[0]
    depth = w_ref.shape[0]
    main = w_ref.shape[1] // 2
    cols = main + e_ref.shape[2]
    rows = 2 * tok // chunks
    piece = tok // share

    barrier = pltpu.get_barrier_semaphore()
    for o in range(1, chips):
        pl.semaphore_signal(barrier, inc=1, device_id=(lax.rem(z + o, chips) * 2 + c, h), device_id_type=MESH)
    pl.semaphore_signal(barrier, inc=1, device_id=(sib, h), device_id_type=MESH)
    for k in range(1, share):
        pl.semaphore_signal(barrier, inc=1, device_id=(f, base + lax.rem(part + k, share)), device_id_type=MESH)
    pl.semaphore_wait(barrier, chips - 1 + 1 + share - 1)

    def spot(chip, core, p):
        return x.at[pl.ds(pl.multiple_of((chip * 2 + core) * tok + p * piece, 16), piece), :]

    def z_copy(o):
        to = lax.rem(z + o, chips)
        src = tok_ref.at[
            pl.ds(pl.multiple_of(part * piece, 16), piece), pl.ds(pl.multiple_of(to * 2 * depth, 128), 2 * depth)
        ]
        return remote(src, spot(z, c, part), z_sem.at[0, o], z_sem.at[1, o], to * 2 + c, h)

    def h_copy(o, k):
        at = spot(lax.rem(z - o + chips, chips), c, part)
        return remote(at, at, h_sem.at[0, o, k], h_sem.at[1, o, k], f, base + lax.rem(part + k, share))

    def s_copy(o, k):
        at = spot(lax.rem(z - o + chips, chips), c, lax.rem(part - k + share, share))
        return remote(at, at, s_sem.at[0, o, k], s_sem.at[1, o, k], sib, h)

    @pl.loop(1, chips)
    def _(o):
        z_copy(o).start()

    mine = tok_ref.at[:, pl.ds(pl.multiple_of(z * 2 * depth, 128), 2 * depth)]
    my_rows = x.at[pl.ds(pl.multiple_of(f * tok, 16), tok), :]
    own = pltpu.make_async_copy(mine, my_rows, local_sem.at[0])
    own.start()
    own_out = remote(mine, my_rows, own_sem.at[0], own_sem.at[1], sib, h)
    own_out.start()
    w_rows = pl.ds(pl.multiple_of(c * depth, 16), depth)
    w_main, w_ext = wv.at[w_rows, pl.ds(0, main)], wv.at[w_rows, pl.ds(main, cols - main)]

    def half_of(core):
        return w_ref.at[:, pl.ds(pl.multiple_of(core * main, 128), main)]

    w_own = pltpu.make_async_copy(half_of(c), w_main, local_sem.at[1])
    w_own.start()
    e_own = pltpu.make_async_copy(e_ref.at[c], w_ext, local_sem.at[2])
    e_own.start()
    w_out = remote(half_of(1 - c), w_main, w_sem.at[0], w_sem.at[1], sib, h)
    w_out.start()
    e_out = remote(e_ref.at[1 - c], w_ext, w_sem.at[2], w_sem.at[3], sib, h)
    e_out.start()

    @pl.loop(1, chips)
    def _(o):
        z_copy(o).wait_recv()
        for k in range(1, share):
            h_copy(o, k).start()
        s_copy(o, 0).start()

    @pl.loop(1, chips)
    def _(o):
        for k in range(1, share):
            h_copy(o, k).wait_recv()
            s_copy(o, k).start()

    own.wait()
    w_own.wait()
    e_own.wait()
    own_out.wait()
    w_out.wait()
    e_out.wait()

    @pl.loop(1, chips)
    def _(o):
        z_copy(o).wait_send()
        for k in range(1, share):
            h_copy(o, k).wait_send()
        for k in range(share):
            s_copy(o, k).wait()

    def partial(d, ch, j):
        left = x[pl.ds(pl.multiple_of(d * 2 * tok + ch * rows, 16), rows), :]
        right = wv[:, pl.ds(pl.multiple_of(j * width, 128), width)]
        return jnp.dot(left, right, preferred_element_type=jnp.float32)

    total = (chips - 1) * chunks

    def line(way, d, ch, i):
        to = z + 1 - 2 * way
        at = buf.at[way, d, pl.ds(pl.multiple_of(ch * rows, 16), rows), :]
        return remote(at, at, line_send.at[way, i], line_recv.at[way, i], to * 2 + c, h)

    def where(way, i):
        d = lax.div(i, chunks)
        return (chips - 1 - d if way == 0 else d), lax.rem(i, chunks)

    @pl.loop(0, total)
    def _(i):
        for way in (0, 1):
            d, ch = where(way, i)
            active = z < d if way == 0 else z > d
            first = z == 0 if way == 0 else z == chips - 1

            @pl.when(active)
            def _(way=way, d=d, ch=ch, first=first):
                at = pl.ds(pl.multiple_of(ch * rows, 16), rows)

                @pl.when(jnp.logical_not(first))
                def _():
                    line(way, d, ch, i).wait_recv()

                    @pl.loop(0, cols // width)
                    def _(j):
                        to = pl.ds(pl.multiple_of(j * width, 128), width)
                        got = buf[way, d, at, to].astype(jnp.float32)
                        buf[way, d, at, to] = (got + partial(d, ch, j)).astype(jnp.bfloat16)

                @pl.when(first)
                def _():
                    @pl.loop(0, cols // width)
                    def _(j):
                        to = pl.ds(pl.multiple_of(j * width, 128), width)
                        buf[way, d, at, to] = partial(d, ch, j).astype(jnp.bfloat16)

                @pl.when(i >= 2)
                def _():
                    d2, ch2 = where(way, i - 2)
                    line(way, d2, ch2, i - 2).wait_send()

                line(way, d, ch, i).start()

    half = chunks // 2

    def finish(ch):
        at = stage.at[pl.ds(pl.multiple_of(lax.rem(ch, half) * rows, 16), rows), :]
        to = out_ref.at[c, pl.ds(pl.multiple_of(lax.rem(ch, half) * rows, 16), rows), :]
        return remote(at, to, fin_sem.at[0, lax.rem(ch, half)], fin_sem.at[1, lax.rem(ch, half)], sib, h)

    @pl.loop(0, chunks)
    def _(ch):
        at = pl.ds(pl.multiple_of(ch * rows, 16), rows)

        @pl.when(z > 0)
        def _():
            line(0, z, ch, (chips - 1 - z) * chunks + ch).wait_recv()

        @pl.when(z < chips - 1)
        def _():
            line(1, z, ch, z * chunks + ch).wait_recv()

        here = lax.div(ch, half) == c
        to_rows = pl.ds(pl.multiple_of(lax.rem(ch, half) * rows, 16), rows)

        @pl.loop(0, cols // width)
        def _(j):
            to = pl.ds(pl.multiple_of(j * width, 128), width)
            stage2 = partial(z, ch, j)

            def both(v):
                @pl.when(here)
                def _():
                    out_ref[c, to_rows, to] = v.astype(jnp.bfloat16)

                @pl.when(jnp.logical_not(here))
                def _():
                    stage[to_rows, to] = v.astype(jnp.bfloat16)

            @pl.when(z == 0)
            def _():
                both(stage2 + buf[1, z, at, to].astype(jnp.float32))

            @pl.when(z == chips - 1)
            def _():
                both(stage2 + buf[0, z, at, to].astype(jnp.float32))

            @pl.when(jnp.logical_and(z > 0, z < chips - 1))
            def _():
                both(stage2 + buf[0, z, at, to].astype(jnp.float32) + buf[1, z, at, to].astype(jnp.float32))

        @pl.when(jnp.logical_not(here))
        def _():
            finish(ch).start()

    @pl.loop(0, half)
    def _(ch):
        finish(ch).wait()

    for way in (0, 1):
        count = (chips - 1 - z if way == 0 else z) * chunks

        @pl.when(count > 0)
        def _(way=way, count=count):
            for back in (2, 1):
                d2, ch2 = where(way, count - back)
                line(way, d2, ch2, count - back).wait_send()


def project(tokens, weights, extra, n_fsdp, n_head):
    chips = n_fsdp // 2
    share = math.gcd(n_head, 4)
    tok = tokens.shape[0]
    depth = weights.shape[0]
    cols = weights.shape[1] // 2 + extra.shape[2]
    chunks = 4
    width = max(w for w in range(128, 769, 128) if cols % w == 0)
    total = (chips - 1) * chunks
    return pl.pallas_call(
        functools.partial(project_kernel, chips, share, chunks, width),
        out_shape=jax.ShapeDtypeStruct((2, tok, cols), jnp.bfloat16),
        in_specs=[pl.BlockSpec(memory_space=pl.ANY)] * 3,
        out_specs=pl.BlockSpec(memory_space=pltpu.VMEM),
        scratch_shapes=[
            pltpu.VMEM((chips * 2 * tok, 2 * depth), jnp.bfloat16),
            pltpu.VMEM((2 * depth, cols), jnp.bfloat16),
            pltpu.VMEM((2, chips, 2 * tok, cols), jnp.bfloat16),
            pltpu.VMEM((tok, cols), jnp.bfloat16),
            pltpu.SemaphoreType.DMA((3,)),
            pltpu.SemaphoreType.DMA((4,)),
            pltpu.SemaphoreType.DMA((2,)),
            pltpu.SemaphoreType.DMA((2, chips)),
            pltpu.SemaphoreType.DMA((2, chips, share)),
            pltpu.SemaphoreType.DMA((2, chips, share)),
            pltpu.SemaphoreType.DMA((2, total)),
            pltpu.SemaphoreType.DMA((2, total)),
            pltpu.SemaphoreType.DMA((2, chunks // 2)),
        ],
        compiler_params=pltpu.CompilerParams(
            collective_id=0, has_side_effects=True, vmem_limit_bytes=48 * 1024 * 1024
        ),
    )(tokens, weights, extra)


def out_kernel(peers, width, n_ref, w_ref, out_ref, wbuf, held, landed, w_sem, send_sem, recv_sem):
    f = lax.axis_index("fsdp")
    h = lax.axis_index("head")
    block = out_ref.shape[1]

    def w_copy(o):
        to = lax.rem(h + o, peers)
        at = w_ref.at[:, pl.ds(pl.multiple_of(to * block, 128), block)]
        return pltpu.make_async_copy(at, wbuf.at[o], w_sem.at[o])

    def send(o):
        return remote(held.at[o], landed.at[o], send_sem.at[o], recv_sem.at[o], f, lax.rem(h + o, peers))

    for o in range(1, peers):
        w_copy(o).start()
    w_copy(0).start()
    barrier = pltpu.get_barrier_semaphore()
    for o in range(1, peers):
        pl.semaphore_signal(barrier, inc=1, device_id=(f, lax.rem(h + o, peers)), device_id_type=MESH)
    pl.semaphore_wait(barrier, peers - 1)

    def columns(o, j):
        to = pl.ds(pl.multiple_of(j * width, 128), width)
        return to, jnp.dot(n_ref[...], wbuf[o, :, to], preferred_element_type=jnp.float32).astype(jnp.bfloat16)

    @pl.loop(1, peers)
    def _(o):
        w_copy(o).wait()

        @pl.loop(0, block // width)
        def _(j):
            to, value = columns(o, j)
            held[o, :, to] = value

        send(o).start()

    w_copy(0).wait()

    @pl.loop(0, block // width)
    def _(j):
        to, value = columns(0, j)
        held[0, :, to] = value

    @pl.loop(1, peers)
    def _(o):
        send(o).wait()

    @pl.loop(0, block // width)
    def _(j):
        to = pl.ds(pl.multiple_of(j * width, 128), width)
        total = held[0, :, to].astype(jnp.float32)
        for o in range(1, peers):
            total = total + landed[o, :, to].astype(jnp.float32)
        out_ref[:, to] = total.astype(jnp.bfloat16)


def out_project(normed, weight, n_head):
    tok, rows = normed.shape
    block = weight.shape[1] // n_head
    width = 256 if block % 256 == 0 else 128
    return pl.pallas_call(
        functools.partial(out_kernel, n_head, width),
        out_shape=jax.ShapeDtypeStruct((tok, block), jnp.bfloat16),
        in_specs=[pl.BlockSpec(memory_space=pltpu.VMEM), pl.BlockSpec(memory_space=pl.ANY)],
        out_specs=pl.BlockSpec(memory_space=pltpu.VMEM),
        scratch_shapes=[
            pltpu.VMEM((n_head, rows, block), jnp.bfloat16),
            pltpu.VMEM((n_head, tok, block), jnp.bfloat16),
            pltpu.VMEM((n_head, tok, block), jnp.bfloat16),
            pltpu.SemaphoreType.DMA((n_head,)),
            pltpu.SemaphoreType.DMA((n_head,)),
            pltpu.SemaphoreType.DMA((n_head,)),
        ],
        compiler_params=pltpu.CompilerParams(
            collective_id=1, has_side_effects=True, vmem_limit_bytes=40 * 1024 * 1024
        ),
    )(normed, weight)


def causal(values, kernel, seq_len):
    columns = values.shape[1]
    seqs = values.reshape(-1, seq_len, columns).astype(jnp.float32)
    taps = kernel.shape[0]
    padded = jnp.pad(seqs, ((0, 0), (taps - 1, 0), (0, 0)))
    total = jnp.zeros(seqs.shape, jnp.float32)
    for tap in range(taps):
        total = total + kernel[tap] * padded[:, tap : tap + seq_len]
    return settle(jax.nn.silu(total).reshape(-1, columns))


def on_device(
    tokens,
    zx_weight,
    dt_weight,
    bc_weight,
    conv_x,
    conv_bc,
    a_log,
    dt_bias,
    d_skip,
    norm_gain,
    out_weight,
):
    tok_rows = tokens.shape[0]
    heads_here = zx_weight.shape[1]
    head_size = zx_weight.shape[2] // 2
    n_head = lax.axis_size("head")
    n_fsdp = lax.axis_size("fsdp")
    head_pos = lax.axis_index("head")
    per_group = n_head // G
    group_id = head_pos // per_group
    group_cols = bc_weight.shape[1] // G
    state = group_cols // 2
    piece_cols = group_cols // per_group
    depth = zx_weight.shape[0]
    bc_part = lax.dynamic_slice_in_dim(bc_weight, head_pos * piece_cols, piece_cols, 1)
    flat_zx = zx_weight.reshape(depth, heads_here * 2 * head_size)
    zx_half, bc_half, dt_half = heads_here * head_size, piece_cols // 2, heads_here // 2
    used = zx_half + bc_half + dt_half
    cols = -(-used // 128) * 128
    blank = jnp.zeros((depth, cols - used), jnp.bfloat16)
    extra = jnp.stack(
        [
            jnp.concatenate(
                [
                    bc_part[:, c * bc_half : (c + 1) * bc_half],
                    dt_weight[:, c * dt_half : (c + 1) * dt_half],
                    blank,
                ],
                axis=1,
            )
            for c in (0, 1)
        ]
    )
    got = project(tokens, flat_zx, extra, n_fsdp, n_head)
    zx = jnp.concatenate([got[0, :, :zx_half], got[1, :, :zx_half]], axis=1).reshape(
        tok_rows, heads_here, 2, head_size
    )
    bc_raw = jnp.concatenate([got[0, :, zx_half : zx_half + bc_half], got[1, :, zx_half : zx_half + bc_half]], axis=1)
    dt_raw = jnp.concatenate([got[0, :, zx_half + bc_half : used], got[1, :, zx_half + bc_half : used]], axis=1)
    if per_group > 1:
        gathered = lax.all_gather(bc_raw, "head", axis=1, tiled=True)
        bc_raw = lax.dynamic_slice_in_dim(gathered, group_id * group_cols, group_cols, 1)
    channels = heads_here * head_size
    gate = zx[:, :, 0, :].astype(jnp.float32).reshape(tok_rows, channels)
    xin = zx[:, :, 1, :].reshape(tok_rows, channels)
    xconv = causal(xin, conv_x, LEN)
    conv_group = lax.dynamic_slice_in_dim(conv_bc, group_id * group_cols, group_cols, 1)
    bconv = causal(bc_raw, conv_group, LEN)
    count = tok_rows // LEN
    steps = jax.nn.softplus(dt_raw.astype(jnp.float32) + dt_bias).reshape(count, LEN, heads_here)
    lower = jnp.arange(LEN)[:, None] >= jnp.arange(LEN)[None, :]
    cum = jnp.einsum(
        "ts,bsh->bth", lower.astype(jnp.float32), -steps * jnp.exp(a_log), precision=lax.Precision.HIGHEST
    )
    seg = cum[:, :, None, :] - cum[:, None, :, :]
    decay = jnp.exp(jnp.where(lower[None, :, :, None], seg, -1e30))
    bseq = bconv[:, :state].reshape(count, LEN, state)
    cseq = bconv[:, state:].reshape(count, LEN, state)
    inner = jnp.einsum("btn,bsn->bts", cseq, bseq, preferred_element_type=jnp.float32)
    weights = inner[..., None] * decay * steps[:, None, :, :]
    xval = xconv.astype(jnp.float32).reshape(count, LEN, heads_here, head_size)
    xbf = xconv.reshape(count, LEN, heads_here, head_size)
    ys = jnp.einsum("btsh,bshp->bthp", weights.astype(jnp.bfloat16), xbf, preferred_element_type=jnp.float32)
    ys = ys + d_skip[None, None, :, None] * xval
    gated = ys.reshape(tok_rows, channels) * jax.nn.silu(gate)
    local_sq = jnp.sum(gated * gated, axis=1)
    if per_group > 1:
        picks = jnp.arange(G)[None, :] == group_id
        totals = lax.psum(jnp.where(picks, local_sq[:, None], 0.0), "head")
        local_sq = jnp.sum(jnp.where(picks, totals, 0.0), axis=1)
    meansq = local_sq / (per_group * channels)
    normed = (gated / jnp.sqrt(meansq + 1e-05)[:, None] * norm_gain).astype(jnp.bfloat16)
    return out_project(normed, out_weight, n_head)


def solution(mesh):
    in_specs = (
        P("fsdp", None),
        P("fsdp", "head", None),
        P("fsdp", "head"),
        P("fsdp", None),
        P(None, "head"),
        P(),
        P("head"),
        P("head"),
        P("head"),
        P("head"),
        P("head", None),
    )
    out_specs = P("fsdp", "head")
    return jax.shard_map(
        on_device, mesh=mesh, in_specs=in_specs, out_specs=out_specs, check_vma=False
    )
```
